512 devices in a mesh: dp: 128 (over z, y, core), vocab: 4 (over x).
Axes of the slice: x: 4, y: 8, z: 8, core: 2. Of those that a mesh axis runs over, the one named last changes fastest.
Arguments:
- hidden: bfloat16 [16384, 18432], P('dp', 'vocab'), may hold values from -24 to 24
- embed_cot: bfloat16 [16384, 18432], P('dp', 'vocab'), may hold values from -24 to 24
- head_block: bfloat16 [128, 18432], P('vocab'), may hold values from -0.125 to 0.125
- lse_rest: float32 [16384], P('dp'), may hold values from 6 to 12
- token_ids: int32 [16384], P('dp'), may hold values from 0 to 255
- target_ids: int32 [16384], P('dp'), may hold values from 0 to 255
Outputs:
- head_grad: bfloat16 [128, 18432], P('vocab')
The draws below stay inside these ranges and needn't reach their ends.
Inputs may be any that keep to these rules, and one draw needn't show every extreme that they name: `token_ids`: ids below 128 are rows of the block, the others lie outside it. `target_ids`: ids below 128 are rows of the block, the others lie outside it.
All inputs are finite; a program needn't handle non-finite values.
Results may differ from the reference program's by a relative error of at most 0.0035.
Values may be sent and summed in bfloat16 or wider, within the bound.
A program may use at most 64 MiB of HBM per device.

```python
import math
import jax
import jax.numpy as jnp
from jax import lax

D = 18432
TOKENS = 16384
BLOCK = 128


def set_ends(values, stream_key, low, high):
    shape = values.shape
    index_at = [jax.random.randint(jax.random.fold_in(stream_key, axis), (), 0, shape[axis]) for axis in range(len(shape))]
    values = values.at[tuple(index_at)].set(low)
    longest = shape.index(max(shape))
    index_at[longest] = (index_at[longest] + 1) % shape[longest]
    return values.at[tuple(index_at)].set(high)


def with_spikes(array, rng, source, target, parts, factor):
    owner, partner = [(jnp.arange(array.shape[position]) // (array.shape[position] // parts)).reshape([-1 if axis == position else 1 for axis in range(array.ndim)]) for position in (source, target)]
    chosen = jax.random.permutation(rng, parts)[partner]
    strong = (owner == chosen) | (owner == (partner + parts // 2) % parts)
    return jnp.where(strong, factor * array, array)


def block_scale(stream_key, shape, pieces, least, top_value):
    factor_of = 1.0
    for position, blocks in pieces:
        draws = jax.random.uniform(jax.random.fold_in(jax.random.fold_in(stream_key, 6), position), (blocks,), jnp.float32, least / len(pieces), top_value / len(pieces))
        factor_of = factor_of * jnp.repeat(jnp.exp(draws), shape[position] // blocks).reshape((-1,) + (1,) * (len(shape) - 1 - position))
    return factor_of


def bell_draw(stream_key, extent, width, most, shards=(), kind=jnp.bfloat16):
    array = width * jax.random.normal(stream_key, extent, jnp.float32)
    if shards:
        array = array * block_scale(stream_key, extent, shards, -0.22, 0.18)
    return jnp.clip(array, -most, most).astype(kind)


def heavy_noise(key, dims, deviation, bound, pieces, heavy, kind=jnp.bfloat16):
    values = deviation * jax.random.normal(key, dims, jnp.float32)
    if pieces:
        values = values * block_scale(key, dims, pieces, -0.22, 0.18)
    return jnp.clip(with_spikes(values, jax.random.fold_in(key, 3), *heavy), -bound, bound).astype(kind)


def setup_inputs(seed: int = 0) -> dict:
    keys = jax.random.split(jax.random.key(seed), 7)
    return {
        "hidden": heavy_noise(keys[0], (TOKENS, D), 1.0, 24.0, ((0, 128), (1, 4)), (0, 1, 128, 5.5)),
        "embed_cot": heavy_noise(keys[1], (TOKENS, D), 1.0, 24.0, ((0, 128), (1, 4)), (0, 1, 128, 5.5)),
        "head_block": bell_draw(keys[2], (BLOCK, D), (D // 9) ** -0.5, 0.125, ((0, 4),)),
        "lse_rest": jnp.clip(6.0 + 6.0 * jax.random.uniform(keys[3], (TOKENS,), jnp.float32) ** block_scale(keys[3], (TOKENS,), ((0, 128),), -0.2, 0.2), 6.0, 12.0),
        "token_ids": set_ends(jax.random.randint(keys[4], (TOKENS,), 0, 2 * BLOCK), jax.random.fold_in(keys[4], 1), 0, (2 * BLOCK) - 1).astype(jnp.int32),
        "target_ids": set_ends(jax.random.randint(keys[5], (TOKENS,), 0, 2 * BLOCK), jax.random.fold_in(keys[5], 1), 0, (2 * BLOCK) - 1).astype(jnp.int32),
    }


def reference(hidden, embed_cot, head_block, lse_rest, token_ids, target_ids):
    block_rows = head_block.shape[0]
    tok_count = hidden.shape[0]
    logits = jnp.dot(hidden, head_block.T, preferred_element_type=jnp.float32)
    exponent = jnp.exp(logits)
    denominator = jnp.exp(lse_rest) + lax.optimization_barrier(jnp.sum(exponent, axis=1))
    vocab_rows = jnp.arange(block_rows, dtype=jnp.int32)
    targets = (target_ids[:, None] == vocab_rows[None, :]).astype(jnp.float32)
    coefficients = (exponent / denominator[:, None] - targets).astype(jnp.bfloat16)
    picks = (token_ids[:, None] == vocab_rows[None, :]).astype(jnp.bfloat16)
    gradient = jnp.dot(coefficients.T, hidden, preferred_element_type=jnp.float32)
    gradient = gradient + jnp.dot(picks.T, embed_cot, preferred_element_type=jnp.float32)
    loss_scale = math.sqrt(block_rows / tok_count)
    return (gradient * loss_scale).astype(jnp.bfloat16)
```

```python
import functools
import math

import jax
import jax.numpy as jnp
from jax import lax
from jax.experimental import pallas as pl
from jax.experimental.pallas import tpu as pltpu
from jax.sharding import PartitionSpec as P

NX, NY, NZ = 4, 8, 8
MESH = pl.DeviceIdType.MESH
SEND_ORDER = (4, 3, 5, 2, 6, 1, 7)
WAIT_ORDER = (1, 7, 2, 6, 3, 5, 4)
BF16, F32 = jnp.bfloat16, jnp.float32


def remote(src, dst, send, recv, device):
    return pltpu.make_async_remote_copy(
        src_ref=src, dst_ref=dst, send_sem=send, recv_sem=recv, device_id=device, device_id_type=MESH
    )


def kernel(
    scale,
    hid, emb, head, lse, tok, tgt,
    out,
    H, E, HB, AUX, LP, RS, XF, G, P1, R1, S2, R2, R3, T, P4,
    loc_sem, sib_s, sib_r, head_s, head_r, rs_s, rs_r, ag_s, ag_r,
    p1_s, p1_r, p2_s, p2_r, p3_s, p3_r, p4_s, p4_r, fw_s, fw_r,
):
    x = lax.axis_index("vocab")
    d = lax.axis_index("dp")
    c, y, z = lax.rem(d, 2), lax.rem(d // 2, NY), d // (2 * NY)
    o = 1 - c
    m = 2 * x + c
    tokens = hid.shape[0]
    rows = head.shape[0]
    cols = hid.shape[1] // 2
    half = cols // 2

    def dev(px, py, pz, pc):
        return ((pz * NY + py) * 2 + pc, px)

    sibling = dev(x, y, z, o)
    ring = (lambda t: lax.rem(y + t, NY), lambda t: lax.rem(z + t, NZ))

    def ring_dev(h, p):
        return dev(x, p, z, c) if h == 0 else dev(x, y, p, c)

    def group_dev(p):
        return dev(p // 2, y, z, lax.rem(p, 2))

    pos = (y, z)
    pos2 = (z, y)

    def second_dev(h, px, p):
        return dev(px, y, p, c) if h == 0 else dev(px, p, z, c)

    own2 = tuple(p // 2 == x for p in pos2)

    mine = pl.ds(pl.multiple_of(c * tokens, tokens), tokens)
    theirs = pl.ds(pl.multiple_of(o * tokens, tokens), tokens)
    my_cols = pl.ds(pl.multiple_of(c * cols, cols), cols)
    their_cols = pl.ds(pl.multiple_of(o * cols, cols), cols)
    my_rows = pl.ds(pl.multiple_of(x * rows, rows), rows)
    locals_ = [
        pltpu.make_async_copy(head.at[:, pl.ds(pl.multiple_of(m * cols, cols), cols)], HB.at[my_rows, :], loc_sem.at[0]),
        pltpu.make_async_copy(hid.at[:, my_cols], H.at[mine, :], loc_sem.at[1]),
        pltpu.make_async_copy(emb.at[:, my_cols], E.at[mine, :], loc_sem.at[2]),
    ]
    for copy in locals_:
        copy.start()

    barrier = pltpu.get_barrier_semaphore()
    for t in range(1, 8):
        pl.semaphore_signal(barrier, inc=1, device_id=group_dev(lax.rem(m + t, 8)), device_id_type=MESH)
    for t in range(1, 8):
        for h in range(2):
            pl.semaphore_signal(barrier, inc=1, device_id=ring_dev(h, ring[h](t)), device_id_type=MESH)
    for h in range(2):
        for s in range(8):
            @pl.when(jnp.logical_not(own2[h] & (pos2[h] == s)))
            def _():
                pl.semaphore_signal(
                    barrier, inc=1, device_id=second_dev(h, pos2[h] // 2, s), device_id_type=MESH
                )

    AUX[mine_block(c), 0:1, :] = lse[...].reshape(1, 1, tokens)
    AUX[mine_block(c), 1:2, :] = tok[...].astype(F32).reshape(1, 1, tokens)
    AUX[mine_block(c), 2:3, :] = tgt[...].astype(F32).reshape(1, 1, tokens)

    pl.semaphore_wait(barrier, 37 - own2[0].astype(jnp.int32) - own2[1].astype(jnp.int32))

    head_copies = []
    for t in (2, 1, 3):
        px = lax.rem(x + t, NX)
        pcols = pl.ds(pl.multiple_of((2 * px + c) * cols, cols), cols)
        copy = remote(head.at[:, pcols], HB.at[my_rows, :], head_s.at[t], head_r.at[t], dev(px, y, z, c))
        copy.start()
        head_copies.append(copy)
    sib = [
        remote(AUX.at[c], AUX.at[c], sib_s.at[0], sib_r.at[0], sibling),
        remote(emb.at[:, their_cols], E.at[mine, :], sib_s.at[1], sib_r.at[1], sibling),
        remote(hid.at[:, their_cols], H.at[mine, :], sib_s.at[2], sib_r.at[2], sibling),
    ]
    for copy in sib:
        copy.start()

    sib_in = [
        remote(AUX.at[o], AUX.at[o], sib_s.at[0], sib_r.at[0], sibling),
        remote(E.at[theirs, :], E.at[theirs, :], sib_s.at[1], sib_r.at[1], sibling),
        remote(H.at[theirs, :], H.at[theirs, :], sib_s.at[2], sib_r.at[2], sibling),
    ]
    sib_in[0].wait_recv()
    sib_in[1].wait_recv()
    locals_[2].wait()
    vocab = NX * rows
    order = lax.broadcasted_iota(jnp.int32, (vocab, tokens), 0)
    ordered = rows * ((order // 4) % 4) + 4 * (order // 16) + order % 4
    ordered = ordered.astype(F32)
    picks = jnp.concatenate(
        [jnp.where(AUX[k, 1:2, :] == ordered, 1.0, 0.0).astype(BF16) for k in range(2)], axis=1
    )
    step = half // 3
    for k in range(6):
        s = slice(k * step, (k + 1) * step)
        G[:, s] = jnp.dot(picks, E[:, s], preferred_element_type=F32)

    sib_in[2].wait_recv()
    locals_[1].wait()
    locals_[0].wait()
    for t in (1, 3, 2):
        src_rows = pl.ds(pl.multiple_of(lax.rem(x + NX - t, NX) * rows, rows), rows)
        remote(HB.at[src_rows, :], HB.at[src_rows, :], head_s.at[t], head_r.at[t], sibling).wait_recv()
    LP[...] = lax.dot_general(HB[...], H[...], (((1,), (1,)), ((), ())), preferred_element_type=F32)

    for t in SEND_ORDER:
        p = lax.rem(m + t, 8)
        remote(
            LP.at[pl.ds(pl.multiple_of(p * 16, 16), 16), :], RS.at[m], rs_s.at[t], rs_r.at[t], group_dev(p)
        ).start()
    my16 = pl.ds(pl.multiple_of(m * 16, 16), 16)
    logits = LP[my16, :]
    for t in WAIT_ORDER:
        p = lax.rem(m + 8 - t, 8)
        remote(RS.at[p], RS.at[p], rs_s.at[t], rs_r.at[t], sibling).wait_recv()
        logits = logits + RS[p]
    XF[my16, :] = jnp.exp(logits)
    for t in SEND_ORDER:
        p = lax.rem(m + t, 8)
        remote(XF.at[my16, :], XF.at[my16, :], ag_s.at[t], ag_r.at[t], group_dev(p)).start()
    natural = lax.broadcasted_iota(jnp.int32, (vocab, tokens), 0).astype(F32)
    swap_r = lax.broadcasted_iota(jnp.int32, (vocab, vocab), 0)
    swap_c = lax.broadcasted_iota(jnp.int32, (vocab, vocab), 1)
    swap = jnp.where(rows * ((swap_r // 4) % 4) + 4 * (swap_r // 16) + swap_r % 4 == swap_c, 1.0, 0.0).astype(BF16)
    for t in WAIT_ORDER:
        p = lax.rem(m + 8 - t, 8)
        p16 = pl.ds(pl.multiple_of(p * 16, 16), 16)
        remote(XF.at[p16, :], XF.at[p16, :], ag_s.at[t], ag_r.at[t], sibling).wait_recv()
    parts = []
    for k in range(2):
        ex = XF[:, k * tokens:(k + 1) * tokens]
        denominator = jnp.exp(AUX[k, 0:1, :]) + jnp.sum(ex, axis=0, keepdims=True)
        coefficients = ex / denominator - jnp.where(AUX[k, 2:3, :] == natural, 1.0, 0.0)
        parts.append(coefficients.astype(BF16))
    coef = jnp.concatenate(parts, axis=1)
    coef = jnp.dot(swap, coef, preferred_element_type=F32).astype(BF16)

    for h in range(2):
        for k in range(3):
            s = slice(h * half + k * step, h * half + (k + 1) * step)
            g = (G[:, s] + jnp.dot(coef, H[:, s], preferred_element_type=F32)) * scale
            G[:, s] = g
            P1[h, :, :, k * step:(k + 1) * step] = g.astype(BF16).reshape(8, 16, step)
        for t in SEND_ORDER:
            p = ring[h](t)
            remote(P1.at[h, p], R1.at[h, pos[h]], p1_s.at[h, t], p1_r.at[h, t], ring_dev(h, p)).start()

    for h in range(2):
        acc = G[pl.ds(pl.multiple_of(pos[h] * 16, 16), 16), h * half:(h + 1) * half]
        for t in WAIT_ORDER:
            p = ring[h](8 - t)
            remote(R1.at[h, p], R1.at[h, p], p1_s.at[h, t], p1_r.at[h, t], sibling).wait_recv()
            acc = acc + R1[h, p].astype(F32)
        for q in range(8):
            S2[h, q] = acc[2 * q:2 * q + 2, :]
        for q in range(8):
            target = 2 * x + q % 2
            is_self = (x == q // 2) & (target == pos2[h])

            @pl.when(jnp.logical_not(is_self))
            def _():
                remote(
                    S2.at[h, q], R2.at[h, pos2[h]], p2_s.at[h, q], p2_r.at[h, pos2[h]],
                    second_dev(h, q // 2, target),
                ).start()

            @pl.when(is_self)
            def _():
                R2[h, pos2[h]] = S2[h, q]

    for h in range(2):
        total = jnp.zeros((2, half), F32)
        for s in range(8):
            @pl.when(jnp.logical_not(own2[h] & (pos2[h] == s)))
            def _():
                remote(R2.at[h, s], R2.at[h, s], p2_s.at[h, s], p2_r.at[h, s], sibling).wait_recv()
        for s in range(8):
            total = total + R2[h, s]
        R3[h, pos2[h]] = total
        for t in SEND_ORDER:
            p = ring[1 - h](t)
            remote(
                R3.at[h, pos2[h]], R3.at[h, pos2[h]], p3_s.at[h, t], p3_r.at[h, t], ring_dev(1 - h, p)
            ).start()

    for h in range(2):
        for t in WAIT_ORDER:
            p = ring[1 - h](8 - t)
            remote(R3.at[h, p], R3.at[h, p], p3_s.at[h, t], p3_r.at[h, t], sibling).wait_recv()
        for k in range(8):
            T[h, 2 * k:2 * k + 2, :] = R3[h, k]
        P4[h] = T[h].astype(BF16)
        for t in SEND_ORDER:
            p = ring[h](t)
            remote(P4.at[h], out.at[h, c, pos[h]], p4_s.at[h, t], p4_r.at[h, t], ring_dev(h, p)).start()
        remote(P4.at[h], out.at[h, c, pos[h]], fw_s.at[h, 0], fw_r.at[h, 0], sibling).start()
        pltpu.make_async_copy(P4.at[h], out.at[h, c, pos[h]], loc_sem.at[3 + h]).start()

    for t in WAIT_ORDER:
        for h in range(2):
            p = ring[h](8 - t)
            slot = out.at[h, c, p]
            remote(slot, slot, p4_s.at[h, t], p4_r.at[h, t], sibling).wait_recv()
            remote(slot, slot, fw_s.at[h, t], fw_r.at[h, t], sibling).start()

    for copy in head_copies + sib:
        copy.wait_send()
    for t in SEND_ORDER:
        remote(RS.at[0], RS.at[0], rs_s.at[t], rs_r.at[t], sibling).wait_send()
        remote(XF.at[my16, :], XF.at[my16, :], ag_s.at[t], ag_r.at[t], sibling).wait_send()
        for h in range(2):
            remote(P1.at[h, 0], R1.at[h, 0], p1_s.at[h, t], p1_r.at[h, t], sibling).wait_send()
            remote(R3.at[h, 0], R3.at[h, 0], p3_s.at[h, t], p3_r.at[h, t], sibling).wait_send()
            remote(P4.at[h], P4.at[h], p4_s.at[h, t], p4_r.at[h, t], sibling).wait_send()
    for h in range(2):
        for q in range(8):
            is_self = (x == q // 2) & (2 * x + q % 2 == pos2[h])

            @pl.when(jnp.logical_not(is_self))
            def _():
                remote(S2.at[h, q], S2.at[h, q], p2_s.at[h, q], p2_r.at[h, q], sibling).wait_send()
        pltpu.make_async_copy(P4.at[h], out.at[h, c, pos[h]], loc_sem.at[3 + h]).wait()
        for t in range(8):
            p = ring[h](8 - t)
            slot = out.at[h, o, p]
            remote(slot, slot, fw_s.at[h, t], fw_r.at[h, t], sibling).wait()


def mine_block(c):
    return pl.ds(c, 1)


def arrange(pieces, result):
    _, _, _, _, half = pieces.shape
    for h in range(2):
        for c in range(2):
            for g in range(2):
                group = [pieces[h, c, 4 * g + j].astype(F32) for j in range(4)]
                for x in range(NX):
                    block = jnp.concatenate([p[4 * x:4 * x + 4, :] for p in group], axis=0)
                    start = (2 * x + c) * 2 * half + h * half
                    result[16 * g:16 * g + 16, start:start + half] = block.astype(BF16)


def local(hidden, embed_cot, head_block, lse_rest, token_ids, target_ids):
    tokens, width = hidden.shape
    rows, model = head_block.shape
    cols, half, vocab = width // 2, width // 4, rows * NX
    scale = math.sqrt(vocab / (tokens * lax.axis_size("dp")))
    hbm = pl.BlockSpec(memory_space=pl.ANY)
    vmem = pl.BlockSpec(memory_space=pltpu.VMEM)
    dma = pltpu.SemaphoreType.DMA
    pieces = pl.pallas_call(
        functools.partial(kernel, scale),
        out_shape=jax.ShapeDtypeStruct((2, 2, 8, 16, half), BF16),
        in_specs=[hbm, hbm, hbm, vmem, vmem, vmem],
        out_specs=hbm,
        scratch_shapes=[
            pltpu.VMEM((2 * tokens, cols), BF16),
            pltpu.VMEM((2 * tokens, cols), BF16),
            pltpu.VMEM((vocab, cols), BF16),
            pltpu.VMEM((2, 8, tokens), F32),
            pltpu.VMEM((vocab, 2 * tokens), F32),
            pltpu.VMEM((8, 16, 2 * tokens), F32),
            pltpu.VMEM((vocab, 2 * tokens), F32),
            pltpu.VMEM((vocab, cols), F32),
            pltpu.VMEM((2, 8, 16, half), BF16),
            pltpu.VMEM((2, 8, 16, half), BF16),
            pltpu.VMEM((2, 8, 2, half), F32),
            pltpu.VMEM((2, 8, 2, half), F32),
            pltpu.VMEM((2, 8, 2, half), F32),
            pltpu.VMEM((2, 16, half), F32),
            pltpu.VMEM((2, 16, half), BF16),
            dma((5,)),
            dma((3,)), dma((3,)),
            dma((4,)), dma((4,)),
            dma((8,)), dma((8,)),
            dma((8,)), dma((8,)),
            dma((2, 8)), dma((2, 8)),
            dma((2, 8)), dma((2, 8)),
            dma((2, 8)), dma((2, 8)),
            dma((2, 8)), dma((2, 8)),
            dma((2, 8)), dma((2, 8)),
        ],
        compiler_params=pltpu.CompilerParams(
            collective_id=0, has_side_effects=True, vmem_limit_bytes=40 * 1024 * 1024
        ),
        name="exchange",
    )(
        hidden, embed_cot, head_block,
        lse_rest.reshape(1, tokens), token_ids.reshape(1, tokens), target_ids.reshape(1, tokens),
    )
    return pl.pallas_call(
        arrange,
        out_shape=jax.ShapeDtypeStruct((rows, model), BF16),
        in_specs=[vmem],
        out_specs=vmem,
        compiler_params=pltpu.CompilerParams(vmem_limit_bytes=40 * 1024 * 1024),
        name="arrange",
    )(pieces)


def solution(mesh):
    return jax.shard_map(
        local,
        mesh=mesh,
        in_specs=(P("dp", "vocab"), P("dp", "vocab"), P("vocab", None), P("dp"), P("dp"), P("dp")),
        out_specs=P("vocab", None),
        check_vma=False,
    )
```

```python
import functools
import math

import jax
import jax.numpy as jnp
from jax import lax
from jax.experimental import pallas as pl
from jax.experimental.pallas import tpu as pltpu
from jax.sharding import PartitionSpec as P

NX, NY, NZ = 4, 8, 8
MESH = pl.DeviceIdType.MESH
SEND_ORDER = (4, 3, 5, 2, 6, 1, 7)
WAIT_ORDER = (1, 7, 2, 6, 3, 5, 4)
CHUNKS = 3
BF16, F32 = jnp.bfloat16, jnp.float32


def remote(src, dst, send, recv, device):
    return pltpu.make_async_remote_copy(
        src_ref=src, dst_ref=dst, send_sem=send, recv_sem=recv, device_id=device, device_id_type=MESH
    )


def kernel(
    scale,
    hid, emb, head, lse, tok, tgt,
    out,
    H, E, HB, LSE, TOK, TGT, LP, RS, XF, G, P1, R1, S2, R2, R3, T, P4,
    loc_sem, out_sem, sib_s, sib_r, head_s, head_r, rs_s, rs_r, ag_s, ag_r,
    p1_s, p1_r, p2_s, p2_r, p3_s, p3_r, p4_s, p4_r, fw_s, fw_r,
):
    x = lax.axis_index("vocab")
    d = lax.axis_index("dp")
    c, y, z = lax.rem(d, 2), lax.rem(d // 2, NY), d // (2 * NY)
    o = 1 - c
    m = 2 * x + c
    tokens = hid.shape[0]
    rows = head.shape[0]
    cols = hid.shape[1] // 2
    half = cols // 2

    def dev(px, py, pz, pc):
        return ((pz * NY + py) * 2 + pc, px)

    sibling = dev(x, y, z, o)
    ring = (lambda t: lax.rem(y + t, NY), lambda t: lax.rem(z + t, NZ))

    def ring_dev(h, p):
        return dev(x, p, z, c) if h == 0 else dev(x, y, p, c)

    def group_dev(p):
        return dev(p // 2, y, z, lax.rem(p, 2))

    pos = (y, z)
    pos2 = (z, y)

    def second_dev(h, px, p):
        return dev(px, y, p, c) if h == 0 else dev(px, p, z, c)

    source = tuple(lax.rem(p // 2 + NX - x, NX) for p in pos2)
    own2 = tuple(p == x for p in source)

    mine = pl.ds(pl.multiple_of(c * tokens, tokens), tokens)
    theirs = pl.ds(pl.multiple_of(o * tokens, tokens), tokens)
    my_cols = pl.ds(pl.multiple_of(c * cols, cols), cols)
    their_cols = pl.ds(pl.multiple_of(o * cols, cols), cols)
    my_rows = pl.ds(pl.multiple_of(x * rows, rows), rows)
    locals_ = [
        pltpu.make_async_copy(head.at[:, pl.ds(pl.multiple_of(m * cols, cols), cols)], HB.at[my_rows, :], loc_sem.at[0]),
        pltpu.make_async_copy(hid.at[:, my_cols], H.at[mine, :], loc_sem.at[1]),
        pltpu.make_async_copy(emb.at[:, my_cols], E.at[mine, :], loc_sem.at[2]),
        pltpu.make_async_copy(tok, TOK.at[c], loc_sem.at[3]),
        pltpu.make_async_copy(lse, LSE.at[c], loc_sem.at[4]),
        pltpu.make_async_copy(tgt, TGT.at[c], loc_sem.at[5]),
    ]
    for copy in locals_:
        copy.start()

    barrier = pltpu.get_barrier_semaphore()
    for t in range(1, 8):
        pl.semaphore_signal(barrier, inc=1, device_id=group_dev(lax.rem(m + t, 8)), device_id_type=MESH)
    for t in range(1, 8):
        for h in range(2):
            pl.semaphore_signal(barrier, inc=1, device_id=ring_dev(h, ring[h](t)), device_id_type=MESH)
    for h in range(2):
        for s in range(8):
            @pl.when(jnp.logical_not(own2[h] & (pos2[h] == s)))
            def _():
                pl.semaphore_signal(
                    barrier, inc=1, device_id=second_dev(h, source[h], s), device_id_type=MESH
                )

    pl.semaphore_wait(barrier, 37 - own2[0].astype(jnp.int32) - own2[1].astype(jnp.int32))

    for t in (2, 1, 3):
        px = lax.rem(x + t, NX)
        pcols = pl.ds(pl.multiple_of((2 * px + c) * cols, cols), cols)
        copy = remote(head.at[:, pcols], HB.at[my_rows, :], head_s, head_r, dev(px, y, z, c))
        copy.start()
    sib = [
        remote(tok, TOK.at[c], sib_s.at[0], sib_r.at[0], sibling),
        remote(lse, LSE.at[c], sib_s.at[3], sib_r.at[3], sibling),
        remote(tgt, TGT.at[c], sib_s.at[4], sib_r.at[4], sibling),
        remote(emb.at[:, their_cols], E.at[mine, :], sib_s.at[1], sib_r.at[1], sibling),
        remote(hid.at[:, their_cols], H.at[mine, :], sib_s.at[2], sib_r.at[2], sibling),
    ]
    for copy in sib:
        copy.start()

    sib_in = [
        remote(TOK.at[o], TOK.at[o], sib_s.at[0], sib_r.at[0], sibling),
        remote(E.at[theirs, :], E.at[theirs, :], sib_s.at[1], sib_r.at[1], sibling),
        remote(H.at[theirs, :], H.at[theirs, :], sib_s.at[2], sib_r.at[2], sibling),
        remote(LSE.at[o], LSE.at[o], sib_s.at[3], sib_r.at[3], sibling),
        remote(TGT.at[o], TGT.at[o], sib_s.at[4], sib_r.at[4], sibling),
    ]
    sib_in[0].wait_recv()
    sib_in[1].wait_recv()
    locals_[2].wait()
    locals_[3].wait()
    vocab = NX * rows
    order = lax.broadcasted_iota(jnp.int32, (vocab, tokens), 0)
    ordered = rows * ((order // 4) % 4) + 4 * (order // 16) + order % 4
    picks = jnp.concatenate(
        [jnp.where(TOK[k] == ordered, 1.0, 0.0).astype(BF16) for k in range(2)], axis=1
    )
    step = half // 3
    for k in range(6):
        s = slice(k * step, (k + 1) * step)
        G[:, s] = jnp.dot(picks, E[:, s], preferred_element_type=F32)

    for copy in sib_in[2:]:
        copy.wait_recv()
    locals_[4].wait()
    locals_[5].wait()
    locals_[1].wait()
    locals_[0].wait()
    heads = remote(HB.at[:(NX - 1) * rows, :], HB.at[:(NX - 1) * rows, :], head_s, head_r, sibling)
    heads.wait_recv()
    LP[...] = lax.dot_general(HB[...], H[...], (((1,), (1,)), ((), ())), preferred_element_type=F32)

    for t in SEND_ORDER:
        p = lax.rem(m + t, 8)
        remote(
            LP.at[pl.ds(pl.multiple_of(p * 16, 16), 16), :], RS.at[m], rs_s, rs_r, group_dev(p)
        ).start()
    my16 = pl.ds(pl.multiple_of(m * 16, 16), 16)
    logits = LP[my16, :]
    remote(RS.at[:7], RS.at[:7], rs_s, rs_r, sibling).wait_recv()
    for t in SEND_ORDER:
        logits = logits + RS[lax.rem(m + t, 8)]
    XF[my16, :] = jnp.exp(logits)
    for t in SEND_ORDER:
        p = lax.rem(m + t, 8)
        remote(XF.at[my16, :], XF.at[my16, :], ag_s, ag_r, group_dev(p)).start()
    natural = lax.broadcasted_iota(jnp.int32, (vocab, tokens), 0)
    swap_r = lax.broadcasted_iota(jnp.int32, (vocab, vocab), 0)
    swap_c = lax.broadcasted_iota(jnp.int32, (vocab, vocab), 1)
    swap = jnp.where(rows * ((swap_r // 4) % 4) + 4 * (swap_r // 16) + swap_r % 4 == swap_c, 1.0, 0.0).astype(BF16)
    remote(XF.at[:7 * 16, :], XF.at[:7 * 16, :], ag_s, ag_r, sibling).wait_recv()
    parts = []
    for k in range(2):
        ex = XF[:, k * tokens:(k + 1) * tokens]
        denominator = jnp.exp(LSE[k]) + jnp.sum(ex, axis=0, keepdims=True)
        coefficients = ex / denominator - jnp.where(TGT[k] == natural, 1.0, 0.0)
        parts.append(coefficients.astype(BF16))
    coef = jnp.concatenate(parts, axis=1)
    coef = jnp.dot(swap, coef, preferred_element_type=F32).astype(BF16)

    chunks = [[(h, k) for h in range(2)] for k in range(CHUNKS)]
    width = half // CHUNKS

    def span(h, k):
        return slice(h * half + k * width, h * half + (k + 1) * width)

    def first(q):
        h, k = q
        s = span(h, k)
        g = (G[:, s] + jnp.dot(coef, H[:, s], preferred_element_type=F32)) * scale
        G[:, s] = g
        P1[h, k] = g.astype(BF16).reshape(8, 16, width)
        for t in SEND_ORDER:
            p = ring[h](t)
            remote(
                P1.at[h, k, p], R1.at[h, k, pos[h]], p1_s.at[h, k], p1_r.at[h, k], ring_dev(h, p)
            ).start()

    def second_waits(q, wait):
        h, k = q
        for n, here in ((7, own2[h]), (8, jnp.logical_not(own2[h]))):
            copy = remote(R2.at[h, k, :n], R2.at[h, k, :n], p2_s.at[h, k], p2_r.at[h, k], sibling)
            pl.when(here)(lambda: wait(copy))

    def second(q):
        h, k = q
        acc = G[pl.ds(pl.multiple_of(pos[h] * 16, 16), 16), span(h, k)]
        remote(R1.at[h, k, :7], R1.at[h, k, :7], p1_s.at[h, k], p1_r.at[h, k], sibling).wait_recv()
        for t in SEND_ORDER:
            acc = acc + R1[h, k, ring[h](t)].astype(F32)
        for i in range(8):
            S2[h, k, i] = acc[2 * i:2 * i + 2, :]
        for r in range(8):
            px = lax.rem(x + r // 2, NX)
            target = 2 * lax.rem(x + px, NX) + r % 2
            i = 2 * px + r % 2
            copy = remote(
                S2.at[h, k, i], R2.at[h, k, pos2[h]], p2_s.at[h, k], p2_r.at[h, k], second_dev(h, px, target)
            )
            if r > 1:
                copy.start()
            else:
                is_self = target == pos2[h]
                pl.when(jnp.logical_not(is_self))(copy.start)

                @pl.when(is_self)
                def _():
                    R2[h, k, pos2[h]] = S2[h, k, i]

    def third(q):
        h, k = q
        second_waits(q, lambda copy: copy.wait_recv())
        total = R2[h, k, 0]
        for s in range(1, 8):
            total = total + R2[h, k, s]
        R3[h, k, pos2[h]] = total
        for t in SEND_ORDER:
            p = ring[1 - h](t)
            remote(
                R3.at[h, k, pos2[h]], R3.at[h, k, pos2[h]], p3_s.at[h, k], p3_r.at[h, k],
                ring_dev(1 - h, p),
            ).start()

    def fourth(q):
        h, k = q
        remote(R3.at[h, k, :7], R3.at[h, k, :7], p3_s.at[h, k], p3_r.at[h, k], sibling).wait_recv()
        for i in range(8):
            T[h, k, 2 * i:2 * i + 2, :] = R3[h, k, i]
        P4[h, k] = T[h, k].astype(BF16)
        slot = out.at[h, c, k, pos[h]]
        for t in SEND_ORDER:
            p = ring[h](t)
            remote(P4.at[h, k], slot, p4_s.at[h, k], p4_r.at[h, k, t], ring_dev(h, p)).start()
        remote(P4.at[h, k], slot, fw_s.at[h, k], fw_r.at[h, k], sibling).start()
        pltpu.make_async_copy(P4.at[h, k], slot, out_sem.at[h, k]).start()

    def fifth(q):
        h, k = q
        for t in WAIT_ORDER:
            slot = out.at[h, c, k, ring[h](8 - t)]
            remote(slot, slot, p4_s.at[h, k], p4_r.at[h, k, t], sibling).wait_recv()
            remote(slot, slot, fw_s.at[h, k], fw_r.at[h, k], sibling).start()

    for step in (first, second, third, fourth, fifth):
        for group in chunks:
            for q in group:
                step(q)

    heads.wait_send()
    for copy in sib:
        copy.wait_send()
    remote(RS.at[:7], RS.at[:7], rs_s, rs_r, sibling).wait_send()
    remote(XF.at[:7 * 16, :], XF.at[:7 * 16, :], ag_s, ag_r, sibling).wait_send()
    for h, k in [q for group in chunks for q in group]:
        remote(P1.at[h, k, :7], P1.at[h, k, :7], p1_s.at[h, k], p1_r.at[h, k], sibling).wait_send()
        remote(R3.at[h, k, :7], R3.at[h, k, :7], p3_s.at[h, k], p3_r.at[h, k], sibling).wait_send()
        remote(P1.at[h, k, :7], P1.at[h, k, :7], p4_s.at[h, k], p4_r.at[h, k, 0], sibling).wait_send()
        second_waits((h, k), lambda copy: copy.wait_send())
        pltpu.make_async_copy(P4.at[h, k], out.at[h, c, k, pos[h]], out_sem.at[h, k]).wait()
        remote(out.at[h, o, k], out.at[h, o, k], fw_s.at[h, k], fw_r.at[h, k], sibling).wait()


def arrange(pieces, result, held, made, in_sem, out_sem):
    width = pieces.shape[-1]
    half = CHUNKS * width
    me = lax.axis_index("vocab")
    places = [(h, c, k) for k in range(CHUNKS) for h in range(2) for c in range(2)]
    loads = [pltpu.make_async_copy(pieces.at[q], held.at[q], in_sem.at[q]) for q in places]
    for copy in loads:
        copy.start()
    stores = []
    for (h, c, k), load in zip(places, loads):
        load.wait()
        for g in range(2):
            group = [held[h, c, k, 4 * g + j].astype(F32) for j in range(4)]
            for x in range(NX):
                block = jnp.concatenate([p[4 * x:4 * x + 4, :] for p in group], axis=0)
                start = (2 * x + c) * 2 * half + h * half + k * width
                made[16 * g:16 * g + 16, start:start + width] = block.astype(BF16)
        for x in range(NX):
            start = (2 * x + c) * 2 * half + h * half + k * width
            place = (2 * lax.rem(x + NX - me, NX) + c) * 2 * half + h * half + k * width
            place = pl.ds(pl.multiple_of(place, 128), width)
            stores.append(
                pltpu.make_async_copy(made.at[:, pl.ds(start, width)], result.at[:, place], out_sem.at[h, c, k, x])
            )
            stores[-1].start()
    for copy in stores:
        copy.wait()


def local(hidden, embed_cot, head_block, lse_rest, token_ids, target_ids):
    tokens, width = hidden.shape
    rows, model = head_block.shape
    cols, width_, vocab = width // 2, width // 4 // CHUNKS, rows * NX
    scale = math.sqrt(vocab / (tokens * lax.axis_size("dp")))
    hbm = pl.BlockSpec(memory_space=pl.ANY)
    dma = pltpu.SemaphoreType.DMA
    pieces = pl.pallas_call(
        functools.partial(kernel, scale),
        out_shape=jax.ShapeDtypeStruct((2, 2, CHUNKS, 8, 16, width_), BF16),
        in_specs=[hbm] * 6,
        out_specs=hbm,
        scratch_shapes=[
            pltpu.VMEM((2 * tokens, cols), BF16),
            pltpu.VMEM((2 * tokens, cols), BF16),
            pltpu.VMEM((vocab, cols), BF16),
            pltpu.VMEM((2, 1, tokens), F32),
            pltpu.VMEM((2, 1, tokens), jnp.int32),
            pltpu.VMEM((2, 1, tokens), jnp.int32),
            pltpu.VMEM((vocab, 2 * tokens), F32),
            pltpu.VMEM((8, 16, 2 * tokens), F32),
            pltpu.VMEM((vocab, 2 * tokens), F32),
            pltpu.VMEM((vocab, cols), F32),
            pltpu.VMEM((2, CHUNKS, 8, 16, width_), BF16),
            pltpu.VMEM((2, CHUNKS, 8, 16, width_), BF16),
            pltpu.VMEM((2, CHUNKS, 8, 2, width_), F32),
            pltpu.VMEM((2, CHUNKS, 8, 2, width_), F32),
            pltpu.VMEM((2, CHUNKS, 8, 2, width_), F32),
            pltpu.VMEM((2, CHUNKS, 16, width_), F32),
            pltpu.VMEM((2, CHUNKS, 16, width_), BF16),
            dma((6,)),
            dma((2, CHUNKS)),
            dma((5,)), dma((5,)),
            dma, dma,
            dma, dma,
            dma, dma,
            dma((2, CHUNKS)), dma((2, CHUNKS)),
            dma((2, CHUNKS)), dma((2, CHUNKS)),
            dma((2, CHUNKS)), dma((2, CHUNKS)),
            dma((2, CHUNKS)), dma((2, CHUNKS, 8)),
            dma((2, CHUNKS)), dma((2, CHUNKS)),
        ],
        compiler_params=pltpu.CompilerParams(
            collective_id=0, has_side_effects=True, vmem_limit_bytes=60 * 1024 * 1024
        ),
        name="exchange",
    )(
        hidden, embed_cot, head_block,
        lse_rest.reshape(1, tokens), token_ids.reshape(1, tokens), target_ids.reshape(1, tokens),
    )
    return pl.pallas_call(
        arrange,
        out_shape=jax.ShapeDtypeStruct((rows, model), BF16),
        in_specs=[hbm],
        out_specs=hbm,
        scratch_shapes=[
            pltpu.VMEM((2, 2, CHUNKS, 8, 16, width_), BF16),
            pltpu.VMEM((rows, model), BF16),
            dma((2, 2, CHUNKS)),
            dma((2, 2, CHUNKS, NX)),
        ],
        compiler_params=pltpu.CompilerParams(vmem_limit_bytes=60 * 1024 * 1024),
        name="arrange",
    )(pieces)


def solution(mesh):
    return jax.shard_map(
        local,
        mesh=mesh,
        in_specs=(P("dp", "vocab"), P("dp", "vocab"), P("vocab", None), P("dp"), P("dp"), P("dp")),
        out_specs=P("vocab", None),
        check_vma=False,
    )
```

```python
import functools
import math

import jax
import jax.numpy as jnp
from jax import lax
from jax.experimental import pallas as pl
from jax.experimental.pallas import tpu as pltpu
from jax.sharding import PartitionSpec as P

NX, NY, NZ = 4, 8, 8
MESH = pl.DeviceIdType.MESH
SEND_ORDER = (4, 3, 5, 2, 6, 1, 7)
CHUNKS = 3
BF16, F32 = jnp.bfloat16, jnp.float32


def remote(src, dst, send, recv, device):
    return pltpu.make_async_remote_copy(
        src_ref=src, dst_ref=dst, send_sem=send, recv_sem=recv, device_id=device, device_id_type=MESH
    )


def kernel(
    scale,
    hid, emb, head, aux,
    out,
    H, E, HB, AUX, LP, RS, XF, G, P1, R1, S2, R2, R3, T,
    loc_sem, sib_s, sib_r, head_s, head_r, rs_s, rs_r, ag_s, ag_r,
    p1_s, p1_r, p2_s, p2_r, p3_s, p3_r, p4_s, p4_r, fw_s, fw_r,
):
    x = lax.axis_index("vocab")
    d = lax.axis_index("dp")
    c, y, z = lax.rem(d, 2), lax.rem(d // 2, NY), d // (2 * NY)
    o = 1 - c
    m = 2 * x + c
    tokens = hid.shape[0]
    rows = head.shape[0]
    cols = hid.shape[1] // 2
    half = cols // 2

    def dev(px, py, pz, pc):
        return ((pz * NY + py) * 2 + pc, px)

    sibling = dev(x, y, z, o)
    ring = (lambda t: lax.rem(y + t, NY), lambda t: lax.rem(z + t, NZ))

    def ring_dev(h, p):
        return dev(x, p, z, c) if h == 0 else dev(x, y, p, c)

    def group_dev(p):
        return dev(p // 2, y, z, lax.rem(p, 2))

    pos = (y, z)
    pos2 = (z, y)

    def second_dev(h, px, p):
        return dev(px, y, p, c) if h == 0 else dev(px, p, z, c)

    source = tuple(lax.rem(p // 2 + NX - x, NX) for p in pos2)
    own2 = tuple(p == x for p in source)

    barrier = pltpu.get_barrier_semaphore()
    for h in range(2):
        for s in range(8):
            @pl.when(jnp.logical_not(own2[h] & (pos2[h] == s)))
            def _():
                pl.semaphore_signal(
                    barrier, inc=1, device_id=second_dev(h, source[h], s), device_id_type=MESH
                )
    for t in SEND_ORDER:
        for h in range(2):
            pl.semaphore_signal(barrier, inc=1, device_id=ring_dev(h, ring[h](t)), device_id_type=MESH)
    for t in SEND_ORDER:
        pl.semaphore_signal(barrier, inc=1, device_id=group_dev(lax.rem(m + t, 8)), device_id_type=MESH)

    mine = pl.ds(pl.multiple_of(c * tokens, tokens), tokens)
    theirs = pl.ds(pl.multiple_of(o * tokens, tokens), tokens)
    my_cols = pl.ds(pl.multiple_of(c * cols, cols), cols)
    their_cols = pl.ds(pl.multiple_of(o * cols, cols), cols)
    my_rows = pl.ds(pl.multiple_of(x * rows, rows), rows)
    locals_ = [
        pltpu.make_async_copy(head.at[:, pl.ds(pl.multiple_of(m * cols, cols), cols)], HB.at[my_rows, :], loc_sem.at[0]),
        pltpu.make_async_copy(hid.at[:, my_cols], H.at[mine, :], loc_sem.at[1]),
        pltpu.make_async_copy(emb.at[:, my_cols], E.at[mine, :], loc_sem.at[2]),
        pltpu.make_async_copy(aux, AUX.at[c], loc_sem.at[3]),
    ]
    for copy in locals_:
        copy.start()

    pl.semaphore_wait(barrier, 37 - own2[0].astype(jnp.int32) - own2[1].astype(jnp.int32))

    for t in (2, 1, 3):
        px = lax.rem(x + t, NX)
        pcols = pl.ds(pl.multiple_of((2 * px + c) * cols, cols), cols)
        copy = remote(head.at[:, pcols], HB.at[my_rows, :], head_s, head_r, dev(px, y, z, c))
        copy.start()
    sib = [
        remote(aux, AUX.at[c], sib_s.at[0], sib_r.at[0], sibling),
        remote(emb.at[:, their_cols], E.at[mine, :], sib_s.at[1], sib_r.at[1], sibling),
        remote(hid.at[:, their_cols], H.at[mine, :], sib_s.at[2], sib_r.at[2], sibling),
    ]
    for copy in sib:
        copy.start()

    sib_in = [
        remote(AUX.at[o], AUX.at[o], sib_s.at[0], sib_r.at[0], sibling),
        remote(E.at[theirs, :], E.at[theirs, :], sib_s.at[1], sib_r.at[1], sibling),
        remote(H.at[theirs, :], H.at[theirs, :], sib_s.at[2], sib_r.at[2], sibling),
    ]
    sib_in[0].wait_recv()
    sib_in[1].wait_recv()
    locals_[2].wait()
    locals_[3].wait()
    vocab = NX * rows
    order = lax.broadcasted_iota(jnp.int32, (vocab, tokens), 0)
    ordered = rows * ((order // 4) % 4) + 4 * (order // 16) + order % 4
    ordered = ordered.astype(F32)
    picks = jnp.concatenate(
        [jnp.where(AUX[k, 1:2, :] == ordered, 1.0, 0.0).astype(BF16) for k in range(2)], axis=1
    )
    step = half // 3
    for k in range(6):
        s = slice(k * step, (k + 1) * step)
        G[:, s] = jnp.dot(picks, E[:, s], preferred_element_type=F32)

    sib_in[2].wait_recv()
    locals_[1].wait()
    locals_[0].wait()
    heads = remote(HB.at[:(NX - 1) * rows, :], HB.at[:(NX - 1) * rows, :], head_s, head_r, sibling)
    heads.wait_recv()
    LP[...] = lax.dot_general(HB[...], H[...], (((1,), (1,)), ((), ())), preferred_element_type=F32)

    for t in SEND_ORDER:
        p = lax.rem(m + t, 8)
        remote(
            LP.at[pl.ds(pl.multiple_of(p * 16, 16), 16), :], RS.at[m], rs_s, rs_r, group_dev(p)
        ).start()
    my16 = pl.ds(pl.multiple_of(m * 16, 16), 16)
    logits = LP[my16, :]
    remote(RS.at[:7], RS.at[:7], rs_s, rs_r, sibling).wait_recv()
    for t in SEND_ORDER:
        logits = logits + RS[lax.rem(m + t, 8)]
    XF[my16, :] = jnp.exp(logits)
    for t in SEND_ORDER:
        p = lax.rem(m + t, 8)
        remote(XF.at[my16, :], XF.at[my16, :], ag_s, ag_r, group_dev(p)).start()
    natural = lax.broadcasted_iota(jnp.int32, (vocab, tokens), 0).astype(F32)
    swap_r = lax.broadcasted_iota(jnp.int32, (vocab, vocab), 0)
    swap_c = lax.broadcasted_iota(jnp.int32, (vocab, vocab), 1)
    swap = jnp.where(rows * ((swap_r // 4) % 4) + 4 * (swap_r // 16) + swap_r % 4 == swap_c, 1.0, 0.0).astype(BF16)
    remote(XF.at[:7 * 16, :], XF.at[:7 * 16, :], ag_s, ag_r, sibling).wait_recv()
    parts = []
    for k in range(2):
        ex = XF[:, k * tokens:(k + 1) * tokens]
        denominator = jnp.exp(AUX[k, 0:1, :]) + jnp.sum(ex, axis=0, keepdims=True)
        coefficients = ex / denominator - jnp.where(AUX[k, 2:3, :] == natural, 1.0, 0.0)
        parts.append(coefficients.astype(BF16))
    coef = jnp.concatenate(parts, axis=1)
    coef = jnp.dot(swap, coef, preferred_element_type=F32).astype(BF16)

    chunks = [[(h, k) for h in range(2)] for k in range(CHUNKS)]
    width = half // CHUNKS

    def span(h, k):
        return slice(h * half + k * width, h * half + (k + 1) * width)

    def first(q):
        h, k = q
        s = span(h, k)
        g = (G[:, s] + jnp.dot(coef, H[:, s], preferred_element_type=F32)) * scale
        G[:, s] = g
        P1[h, k] = g.astype(BF16).reshape(8, 16, width)
        for t in SEND_ORDER:
            p = ring[h](t)
            remote(
                P1.at[h, k, p], R1.at[h, k, pos[h]], p1_s.at[h, k], p1_r.at[h, k], ring_dev(h, p)
            ).start()

    def second_waits(q, wait):
        h, k = q
        for n, here in ((7, own2[h]), (8, jnp.logical_not(own2[h]))):
            copy = remote(R2.at[h, k, :n], R2.at[h, k, :n], p2_s.at[h, k], p2_r.at[h, k], sibling)
            pl.when(here)(lambda: wait(copy))

    def second(q):
        h, k = q
        acc = G[pl.ds(pl.multiple_of(pos[h] * 16, 16), 16), span(h, k)]
        remote(R1.at[h, k, :7], R1.at[h, k, :7], p1_s.at[h, k], p1_r.at[h, k], sibling).wait_recv()
        for t in SEND_ORDER:
            acc = acc + R1[h, k, ring[h](t)].astype(F32)
        for i in range(8):
            S2[h, k, i] = acc[2 * i:2 * i + 2, :]
        for r in range(8):
            px = lax.rem(x + r // 2, NX)
            target = 2 * lax.rem(x + px, NX) + r % 2
            i = 2 * px + r % 2
            copy = remote(
                S2.at[h, k, i], R2.at[h, k, pos2[h]], p2_s.at[h, k], p2_r.at[h, k], second_dev(h, px, target)
            )
            if r > 1:
                copy.start()
            else:
                is_self = target == pos2[h]
                pl.when(jnp.logical_not(is_self))(copy.start)

                @pl.when(is_self)
                def _():
                    R2[h, k, pos2[h]] = S2[h, k, i]

    def third(q):
        h, k = q
        second_waits(q, lambda copy: copy.wait_recv())
        total = R2[h, k, 0]
        for s in range(1, 8):
            total = total + R2[h, k, s]
        R3[h, k, pos2[h]] = total
        for t in SEND_ORDER:
            p = ring[1 - h](t)
            remote(
                R3.at[h, k, pos2[h]], R3.at[h, k, pos2[h]], p3_s.at[h, k], p3_r.at[h, k],
                ring_dev(1 - h, p),
            ).start()

    def fourth(q):
        h, k = q
        remote(R3.at[h, k, :7], R3.at[h, k, :7], p3_s.at[h, k], p3_r.at[h, k], sibling).wait_recv()
        for i in range(8):
            T[h, k, 2 * i:2 * i + 2, :] = R3[h, k, i]
        out[h, c, k, pos[h]] = T[h, k].astype(BF16)
        slot = out.at[h, c, k, pos[h]]
        for t in SEND_ORDER:
            remote(slot, slot, p4_s.at[h, k], p4_r.at[h, k], ring_dev(h, ring[h](t))).start()

    def fifth(q):
        h, k = q
        seven = out.at[h, c, k, :7]
        remote(seven, seven, p4_s.at[h, k], p4_r.at[h, k], sibling).wait_recv()
        remote(out.at[h, c, k], out.at[h, c, k], fw_s.at[h, k], fw_r.at[h, k], sibling).start()

    for step in (first, second, third, fourth, fifth):
        for group in chunks:
            for q in group:
                step(q)

    heads.wait_send()
    for copy in sib:
        copy.wait_send()
    remote(RS.at[:7], RS.at[:7], rs_s, rs_r, sibling).wait_send()
    remote(XF.at[:7 * 16, :], XF.at[:7 * 16, :], ag_s, ag_r, sibling).wait_send()
    for h, k in [q for group in chunks for q in group]:
        seven = P1.at[h, k, :7]
        remote(seven, seven, p1_s.at[h, k], p1_r.at[h, k], sibling).wait_send()
        remote(R3.at[h, k, :7], R3.at[h, k, :7], p3_s.at[h, k], p3_r.at[h, k], sibling).wait_send()
        remote(P1.at[h, k, :7], P1.at[h, k, :7], p4_s.at[h, k], p4_r.at[h, k], sibling).wait_send()
        second_waits((h, k), lambda copy: copy.wait_send())
        remote(out.at[h, o, k], out.at[h, o, k], fw_s.at[h, k], fw_r.at[h, k], sibling).wait()


def arrange(pieces, result, made, out_sem):
    width = pieces.shape[-1]
    half = CHUNKS * width
    me = lax.axis_index("vocab")
    places = [(h, c, k) for k in range(CHUNKS) for h in range(2) for c in range(2)]
    stores = []
    for h, c, k in places:
        for g in range(2):
            group = [pieces[h, c, k, 4 * g + j].astype(F32) for j in range(4)]
            for x in range(NX):
                block = jnp.concatenate([p[4 * x:4 * x + 4, :] for p in group], axis=0)
                start = (2 * x + c) * 2 * half + h * half + k * width
                made[16 * g:16 * g + 16, start:start + width] = block.astype(BF16)
        for x in range(NX):
            start = (2 * x + c) * 2 * half + h * half + k * width
            place = (2 * lax.rem(x + NX - me, NX) + c) * 2 * half + h * half + k * width
            place = pl.ds(pl.multiple_of(place, 128), width)
            stores.append(
                pltpu.make_async_copy(made.at[:, pl.ds(start, width)], result.at[:, place], out_sem.at[h, c, k, x])
            )
            stores[-1].start()
    for copy in stores:
        copy.wait()


def local(hidden, embed_cot, head_block, lse_rest, token_ids, target_ids):
    tokens, width = hidden.shape
    rows, model = head_block.shape
    cols, width_, vocab = width // 2, width // 4 // CHUNKS, rows * NX
    scale = math.sqrt(vocab / (tokens * lax.axis_size("dp")))
    line = lax.broadcasted_iota(jnp.int32, (3, tokens), 0)
    ids = jnp.where(line == 1, token_ids[None, :], target_ids[None, :]).astype(F32)
    aux = jnp.where(line == 0, lse_rest[None, :], ids)
    hbm = pl.BlockSpec(memory_space=pltpu.HBM)
    vmem = pl.BlockSpec(memory_space=pltpu.VMEM)
    dma = pltpu.SemaphoreType.DMA
    pieces = pl.pallas_call(
        functools.partial(kernel, scale),
        out_shape=jax.ShapeDtypeStruct((2, 2, CHUNKS, 8, 16, width_), BF16),
        in_specs=[hbm] * 4,
        out_specs=vmem,
        scratch_shapes=[
            pltpu.VMEM((2 * tokens, cols), BF16),
            pltpu.VMEM((2 * tokens, cols), BF16),
            pltpu.VMEM((vocab, cols), BF16),
            pltpu.VMEM((2, 3, tokens), F32),
            pltpu.VMEM((vocab, 2 * tokens), F32),
            pltpu.VMEM((8, 16, 2 * tokens), F32),
            pltpu.VMEM((vocab, 2 * tokens), F32),
            pltpu.VMEM((vocab, cols), F32),
            pltpu.VMEM((2, CHUNKS, 8, 16, width_), BF16),
            pltpu.VMEM((2, CHUNKS, 8, 16, width_), BF16),
            pltpu.VMEM((2, CHUNKS, 8, 2, width_), F32),
            pltpu.VMEM((2, CHUNKS, 8, 2, width_), F32),
            pltpu.VMEM((2, CHUNKS, 8, 2, width_), F32),
            pltpu.VMEM((2, CHUNKS, 16, width_), F32),
            dma((4,)),
            dma((3,)), dma((3,)),
            dma, dma,
            dma, dma,
            dma, dma,
            dma((2, CHUNKS)), dma((2, CHUNKS)),
            dma((2, CHUNKS)), dma((2, CHUNKS)),
            dma((2, CHUNKS)), dma((2, CHUNKS)),
            dma((2, CHUNKS)), dma((2, CHUNKS)),
            dma((2, CHUNKS)), dma((2, CHUNKS)),
        ],
        compiler_params=pltpu.CompilerParams(
            collective_id=0, has_side_effects=True, vmem_limit_bytes=52 * 1024 * 1024
        ),
        name="exchange",
    )(
        hidden, embed_cot, head_block,
        aux,
    )
    return pl.pallas_call(
        arrange,
        out_shape=jax.ShapeDtypeStruct((rows, model), BF16),
        in_specs=[vmem],
        out_specs=hbm,
        scratch_shapes=[
            pltpu.VMEM((rows, model), BF16),
            dma((2, 2, CHUNKS, NX)),
        ],
        compiler_params=pltpu.CompilerParams(vmem_limit_bytes=16 * 1024 * 1024),
        name="arrange",
    )(pieces)


def solution(mesh):
    return jax.shard_map(
        local,
        mesh=mesh,
        in_specs=(P("dp", "vocab"), P("dp", "vocab"), P("vocab", None), P("dp"), P("dp"), P("dp")),
        out_specs=P("vocab", None),
        check_vma=False,
    )
```

```python
import functools
import math

import jax
import jax.numpy as jnp
from jax import lax
from jax.experimental import pallas as pl
from jax.experimental.pallas import tpu as pltpu
from jax.sharding import PartitionSpec as P

NX, NY, NZ = 4, 8, 8
MESH = pl.DeviceIdType.MESH
SEND_ORDER = (4, 3, 5, 2, 6, 1, 7)
CHUNKS = 3
BF16, F32 = jnp.bfloat16, jnp.float32


def remote(src, dst, send, recv, device):
    return pltpu.make_async_remote_copy(
        src_ref=src, dst_ref=dst, send_sem=send, recv_sem=recv, device_id=device, device_id_type=MESH
    )


def kernel(
    scale,
    hid, emb, head, aux,
    out,
    H, E, HB, AUX, LP, RS, XF, G, P1, R1, S2, R2, R3, T,
    loc_sem, sib_s, sib_r, head_s, head_r, rs_s, rs_r, ag_s, ag_r,
    p1_s, p1_r, p2_s, p2_r, p3_s, p3_r, p4_s, p4_r, fw_s, fw_r,
):
    x = lax.axis_index("vocab")
    d = lax.axis_index("dp")
    c, y, z = lax.rem(d, 2), lax.rem(d // 2, NY), d // (2 * NY)
    o = 1 - c
    m = 2 * x + c
    tokens = hid.shape[0]
    rows = head.shape[0]
    cols = hid.shape[1] // 2
    half = cols // 2

    def dev(px, py, pz, pc):
        return ((pz * NY + py) * 2 + pc, px)

    sibling = dev(x, y, z, o)
    ring = (lambda t: lax.rem(y + t, NY), lambda t: lax.rem(z + t, NZ))

    def ring_dev(h, p):
        return dev(x, p, z, c) if h == 0 else dev(x, y, p, c)

    def group_dev(p):
        return dev(p // 2, y, z, lax.rem(p, 2))

    pos = (y, z)
    pos2 = (z, y)

    def second_dev(h, px, p):
        return dev(px, y, p, c) if h == 0 else dev(px, p, z, c)

    source = tuple(lax.rem(p // 2 + NX - x, NX) for p in pos2)
    own2 = tuple(p == x for p in source)

    barrier = pltpu.get_barrier_semaphore()
    for h in range(2):
        for s in range(8):
            @pl.when(jnp.logical_not(own2[h] & (pos2[h] == s)))
            def _():
                pl.semaphore_signal(
                    barrier, inc=1, device_id=second_dev(h, source[h], s), device_id_type=MESH
                )
    for t in SEND_ORDER:
        for h in range(2):
            pl.semaphore_signal(barrier, inc=1, device_id=ring_dev(h, ring[h](t)), device_id_type=MESH)
    for t in SEND_ORDER:
        pl.semaphore_signal(barrier, inc=1, device_id=group_dev(lax.rem(m + t, 8)), device_id_type=MESH)

    mine = pl.ds(pl.multiple_of(c * tokens, tokens), tokens)
    theirs = pl.ds(pl.multiple_of(o * tokens, tokens), tokens)
    my_cols = pl.ds(pl.multiple_of(c * cols, cols), cols)
    their_cols = pl.ds(pl.multiple_of(o * cols, cols), cols)
    my_rows = pl.ds(pl.multiple_of(x * rows, rows), rows)
    locals_ = [
        pltpu.make_async_copy(head.at[:, pl.ds(pl.multiple_of(m * cols, cols), cols)], HB.at[my_rows, :], loc_sem.at[0]),
        pltpu.make_async_copy(hid.at[:, my_cols], H.at[mine, :], loc_sem.at[1]),
        pltpu.make_async_copy(emb.at[:, my_cols], E.at[mine, :], loc_sem.at[2]),
        pltpu.make_async_copy(aux, AUX.at[c], loc_sem.at[3]),
    ]
    for copy in locals_:
        copy.start()

    pl.semaphore_wait(barrier, 37 - own2[0].astype(jnp.int32) - own2[1].astype(jnp.int32))

    sib = [
        remote(aux, AUX.at[c], sib_s.at[0], sib_r.at[0], sibling),
        remote(emb.at[:, their_cols], E.at[mine, :], sib_s.at[1], sib_r.at[1], sibling),
        remote(hid.at[:, their_cols], H.at[mine, :], sib_s.at[2], sib_r.at[2], sibling),
    ]
    for copy in sib:
        copy.start()
    for t in (2, 1, 3):
        px = lax.rem(x + t, NX)
        pcols = pl.ds(pl.multiple_of((2 * px + c) * cols, cols), cols)
        copy = remote(head.at[:, pcols], HB.at[my_rows, :], head_s, head_r, dev(px, y, z, c))
        copy.start()

    sib_in = [
        remote(AUX.at[o], AUX.at[o], sib_s.at[0], sib_r.at[0], sibling),
        remote(E.at[theirs, :], E.at[theirs, :], sib_s.at[1], sib_r.at[1], sibling),
        remote(H.at[theirs, :], H.at[theirs, :], sib_s.at[2], sib_r.at[2], sibling),
    ]
    sib_in[0].wait_recv()
    sib_in[1].wait_recv()
    locals_[2].wait()
    locals_[3].wait()
    vocab = NX * rows
    order = lax.broadcasted_iota(jnp.int32, (vocab, tokens), 0)
    ordered = rows * ((order // 4) % 4) + 4 * (order // 16) + order % 4
    ordered = ordered.astype(F32)
    picks = jnp.concatenate(
        [jnp.where(AUX[k, 1:2, :] == ordered, 1.0, 0.0).astype(BF16) for k in range(2)], axis=1
    )
    step = half // 3
    for k in range(6):
        s = slice(k * step, (k + 1) * step)
        G[:, s] = jnp.dot(picks, E[:, s], preferred_element_type=F32)

    sib_in[2].wait_recv()
    locals_[1].wait()
    locals_[0].wait()
    heads = remote(HB.at[:(NX - 1) * rows, :], HB.at[:(NX - 1) * rows, :], head_s, head_r, sibling)
    heads.wait_recv()
    LP[...] = lax.dot_general(HB[...], H[...], (((1,), (1,)), ((), ())), preferred_element_type=F32)

    for t in SEND_ORDER:
        p = lax.rem(m + t, 8)
        remote(
            LP.at[pl.ds(pl.multiple_of(p * 16, 16), 16), :], RS.at[m], rs_s, rs_r, group_dev(p)
        ).start()
    my16 = pl.ds(pl.multiple_of(m * 16, 16), 16)
    logits = LP[my16, :]
    remote(RS.at[:7], RS.at[:7], rs_s, rs_r, sibling).wait_recv()
    for t in SEND_ORDER:
        logits = logits + RS[lax.rem(m + t, 8)]
    XF[my16, :] = jnp.exp(logits)
    for t in SEND_ORDER:
        p = lax.rem(m + t, 8)
        remote(XF.at[my16, :], XF.at[my16, :], ag_s, ag_r, group_dev(p)).start()
    natural = lax.broadcasted_iota(jnp.int32, (vocab, tokens), 0).astype(F32)
    swap_r = lax.broadcasted_iota(jnp.int32, (vocab, vocab), 0)
    swap_c = lax.broadcasted_iota(jnp.int32, (vocab, vocab), 1)
    swap = jnp.where(rows * ((swap_r // 4) % 4) + 4 * (swap_r // 16) + swap_r % 4 == swap_c, 1.0, 0.0).astype(BF16)
    remote(XF.at[:7 * 16, :], XF.at[:7 * 16, :], ag_s, ag_r, sibling).wait_recv()
    parts = []
    for k in range(2):
        ex = XF[:, k * tokens:(k + 1) * tokens]
        denominator = jnp.exp(AUX[k, 0:1, :]) + jnp.sum(ex, axis=0, keepdims=True)
        coefficients = ex / denominator - jnp.where(AUX[k, 2:3, :] == natural, 1.0, 0.0)
        parts.append(coefficients.astype(BF16))
    coef = jnp.concatenate(parts, axis=1)
    coef = jnp.dot(swap, coef, preferred_element_type=F32).astype(BF16)

    chunks = [[(h, k) for h in range(2)] for k in range(CHUNKS)]
    width = half // CHUNKS

    def span(h, k):
        return slice(h * half + k * width, h * half + (k + 1) * width)

    def first(q):
        h, k = q
        s = span(h, k)
        g = (G[:, s] + jnp.dot(coef, H[:, s], preferred_element_type=F32)) * scale
        G[:, s] = g
        P1[h, k] = g.astype(BF16).reshape(8, 16, width)
        for t in SEND_ORDER:
            p = ring[h](t)
            remote(
                P1.at[h, k, p], R1.at[h, k, pos[h]], p1_s.at[h, k], p1_r.at[h, k], ring_dev(h, p)
            ).start()

    def second_waits(q, wait):
        h, k = q
        for n, here in ((7, own2[h]), (8, jnp.logical_not(own2[h]))):
            copy = remote(R2.at[h, k, :n], R2.at[h, k, :n], p2_s.at[h, k], p2_r.at[h, k], sibling)
            pl.when(here)(lambda: wait(copy))

    def second(q):
        h, k = q
        acc = G[pl.ds(pl.multiple_of(pos[h] * 16, 16), 16), span(h, k)]
        remote(R1.at[h, k, :7], R1.at[h, k, :7], p1_s.at[h, k], p1_r.at[h, k], sibling).wait_recv()
        for t in SEND_ORDER:
            acc = acc + R1[h, k, ring[h](t)].astype(F32)
        for i in range(8):
            S2[h, k, i] = acc[2 * i:2 * i + 2, :]
        for r in range(8):
            px = lax.rem(x + r // 2, NX)
            target = 2 * lax.rem(x + px, NX) + r % 2
            i = 2 * px + r % 2
            copy = remote(
                S2.at[h, k, i], R2.at[h, k, pos2[h]], p2_s.at[h, k], p2_r.at[h, k], second_dev(h, px, target)
            )
            if r > 1:
                copy.start()
            else:
                is_self = target == pos2[h]
                pl.when(jnp.logical_not(is_self))(copy.start)

                @pl.when(is_self)
                def _():
                    R2[h, k, pos2[h]] = S2[h, k, i]

    def third(q):
        h, k = q
        second_waits(q, lambda copy: copy.wait_recv())
        total = R2[h, k, 0]
        for s in range(1, 8):
            total = total + R2[h, k, s]
        R3[h, k, pos2[h]] = total
        for t in SEND_ORDER:
            p = ring[1 - h](t)
            remote(
                R3.at[h, k, pos2[h]], R3.at[h, k, pos2[h]], p3_s.at[h, k], p3_r.at[h, k],
                ring_dev(1 - h, p),
            ).start()

    def fourth(q):
        h, k = q
        remote(R3.at[h, k, :7], R3.at[h, k, :7], p3_s.at[h, k], p3_r.at[h, k], sibling).wait_recv()
        for i in range(8):
            T[h, k, 2 * i:2 * i + 2, :] = R3[h, k, i]
        out[h, c, k, pos[h]] = T[h, k].astype(BF16)
        slot = out.at[h, c, k, pos[h]]
        for t in SEND_ORDER:
            remote(slot, slot, p4_s.at[h, k], p4_r.at[h, k], ring_dev(h, ring[h](t))).start()

    def fifth(q):
        h, k = q
        seven = out.at[h, c, k, :7]
        remote(seven, seven, p4_s.at[h, k], p4_r.at[h, k], sibling).wait_recv()
        remote(out.at[h, c, k], out.at[h, c, k], fw_s.at[h, k], fw_r.at[h, k], sibling).start()

    for step in (first, second, third, fourth, fifth):
        for group in chunks:
            for q in group:
                step(q)

    heads.wait_send()
    for copy in sib:
        copy.wait_send()
    remote(RS.at[:7], RS.at[:7], rs_s, rs_r, sibling).wait_send()
    remote(XF.at[:7 * 16, :], XF.at[:7 * 16, :], ag_s, ag_r, sibling).wait_send()
    for h, k in [q for group in chunks for q in group]:
        seven = P1.at[h, k, :7]
        remote(seven, seven, p1_s.at[h, k], p1_r.at[h, k], sibling).wait_send()
        remote(R3.at[h, k, :7], R3.at[h, k, :7], p3_s.at[h, k], p3_r.at[h, k], sibling).wait_send()
        remote(P1.at[h, k, :7], P1.at[h, k, :7], p4_s.at[h, k], p4_r.at[h, k], sibling).wait_send()
        second_waits((h, k), lambda copy: copy.wait_send())
        remote(out.at[h, o, k], out.at[h, o, k], fw_s.at[h, k], fw_r.at[h, k], sibling).wait()


def arrange(pieces, result, made, out_sem):
    width = pieces.shape[-1]
    half = CHUNKS * width
    me = lax.axis_index("vocab")
    places = [(h, c, k) for k in range(CHUNKS) for h in range(2) for c in range(2)]
    stores = []
    for h, c, k in places:
        for g in range(2):
            group = [pieces[h, c, k, 4 * g + j].astype(F32) for j in range(4)]
            for x in range(NX):
                block = jnp.concatenate([p[4 * x:4 * x + 4, :] for p in group], axis=0)
                start = (2 * x + c) * 2 * half + h * half + k * width
                made[16 * g:16 * g + 16, start:start + width] = block.astype(BF16)
        for x in range(NX):
            start = (2 * x + c) * 2 * half + h * half + k * width
            place = (2 * lax.rem(x + NX - me, NX) + c) * 2 * half + h * half + k * width
            place = pl.ds(pl.multiple_of(place, 128), width)
            stores.append(
                pltpu.make_async_copy(made.at[:, pl.ds(start, width)], result.at[:, place], out_sem.at[h, c, k, x])
            )
            stores[-1].start()
    for copy in stores:
        copy.wait()


def local(hidden, embed_cot, head_block, lse_rest, token_ids, target_ids):
    tokens, width = hidden.shape
    rows, model = head_block.shape
    cols, width_, vocab = width // 2, width // 4 // CHUNKS, rows * NX
    scale = math.sqrt(vocab / (tokens * lax.axis_size("dp")))
    ids = jnp.pad(token_ids[None], ((1, 1), (0, 0))) + jnp.pad(target_ids[None], ((2, 0), (0, 0)))
    aux = jnp.pad(lse_rest[None], ((0, 2), (0, 0))) + ids.astype(F32)
    hbm = pl.BlockSpec(memory_space=pltpu.HBM)
    vmem = pl.BlockSpec(memory_space=pltpu.VMEM)
    dma = pltpu.SemaphoreType.DMA
    pieces = pl.pallas_call(
        functools.partial(kernel, scale),
        out_shape=jax.ShapeDtypeStruct((2, 2, CHUNKS, 8, 16, width_), BF16),
        in_specs=[hbm] * 4,
        out_specs=vmem,
        scratch_shapes=[
            pltpu.VMEM((2 * tokens, cols), BF16),
            pltpu.VMEM((2 * tokens, cols), BF16),
            pltpu.VMEM((vocab, cols), BF16),
            pltpu.VMEM((2, 3, tokens), F32),
            pltpu.VMEM((vocab, 2 * tokens), F32),
            pltpu.VMEM((8, 16, 2 * tokens), F32),
            pltpu.VMEM((vocab, 2 * tokens), F32),
            pltpu.VMEM((vocab, cols), F32),
            pltpu.VMEM((2, CHUNKS, 8, 16, width_), BF16),
            pltpu.VMEM((2, CHUNKS, 8, 16, width_), BF16),
            pltpu.VMEM((2, CHUNKS, 8, 2, width_), F32),
            pltpu.VMEM((2, CHUNKS, 8, 2, width_), F32),
            pltpu.VMEM((2, CHUNKS, 8, 2, width_), F32),
            pltpu.VMEM((2, CHUNKS, 16, width_), F32),
            dma((4,)),
            dma((3,)), dma((3,)),
            dma, dma,
            dma, dma,
            dma, dma,
            dma((2, CHUNKS)), dma((2, CHUNKS)),
            dma((2, CHUNKS)), dma((2, CHUNKS)),
            dma((2, CHUNKS)), dma((2, CHUNKS)),
            dma((2, CHUNKS)), dma((2, CHUNKS)),
            dma((2, CHUNKS)), dma((2, CHUNKS)),
        ],
        compiler_params=pltpu.CompilerParams(
            collective_id=0, has_side_effects=True, vmem_limit_bytes=52 * 1024 * 1024
        ),
        name="exchange",
    )(
        hidden, embed_cot, head_block,
        aux,
    )
    return pl.pallas_call(
        arrange,
        out_shape=jax.ShapeDtypeStruct((rows, model), BF16),
        in_specs=[vmem],
        out_specs=hbm,
        scratch_shapes=[
            pltpu.VMEM((rows, model), BF16),
            dma((2, 2, CHUNKS, NX)),
        ],
        compiler_params=pltpu.CompilerParams(vmem_limit_bytes=16 * 1024 * 1024),
        name="arrange",
    )(pieces)


def solution(mesh):
    return jax.shard_map(
        local,
        mesh=mesh,
        in_specs=(P("dp", "vocab"), P("dp", "vocab"), P("vocab", None), P("dp"), P("dp"), P("dp")),
        out_specs=P("vocab", None),
        check_vma=False,
    )
```
